32 devices in a mesh: parts: 2 (over x), fibre: 16 (over z, y, core).
Axes of the slice: x: 2, y: 2, z: 4, core: 2. Of those that a mesh axis runs over, the one named last changes fastest.
Arguments:
- signal: bfloat16 [64, 16, 8192], P('parts', None, 'fibre'), parts along dimension 0, may hold values from -6 to 6
- conv_taps: bfloat16 [5, 5, 64, 32], replicated, may hold values from -0.21875 to 0.21875
- response: float32 [2, 64, 4096], P(None, 'fibre'), may hold values from -4 to 4
- cotangent: bfloat16 [128, 8, 4096], P('parts', None, 'fibre'), parts along dimension 0, may hold values from -6 to 6
Outputs:
- input_grad: bfloat16 [64, 16, 8192], P('parts', None, 'fibre'), parts along dimension 0
- tap_grad: float32 [10, 5, 64, 32], P('parts'), parts along dimension 0
- filter_grad: float32 [4, 64, 4096], P('parts', 'fibre'), parts along dimension 0
The draws below stay inside these ranges and needn't reach their ends.
There are 2 independent parts, one for each index of `parts`. The reference program is written for one: setup_inputs(seed, part) draws one part's arguments, and reference() takes and returns one part's arrays. A program takes and returns all parts, laid end to end along the dimension named above; an argument that names none is the same for every part. Nothing has to cross between parts.
All inputs are finite; a program needn't handle non-finite values.
Results may differ from the reference program's by a relative error of at most 0.012.
Values may be sent and summed in bfloat16 or wider, within the bound.
A program may use at most 64 MiB of HBM per device.

```python
import math
import jax
import jax.numpy as jnp
from jax import lax

CIN = 32
COUT = 64
KS = 5
TW = 16
TH = 8
FIB = 8192
KH = 4096


def block_scale(stream_key, dims, cuts, least, largest):
    loudness = 1.0
    for axis_at, shards_of in cuts:
        steps = jax.random.uniform(jax.random.fold_in(jax.random.fold_in(stream_key, 6), axis_at), (shards_of,), jnp.float32, least / len(cuts), largest / len(cuts))
        loudness = loudness * jnp.repeat(jnp.exp(steps), dims[axis_at] // shards_of).reshape((-1,) + (1,) * (len(dims) - 1 - axis_at))
    return loudness


def bell_draw(own_key, extent, width, most, shards=(), held_as=jnp.bfloat16):
    array = width * jax.random.normal(own_key, extent, jnp.float32)
    if shards:
        array = array * block_scale(own_key, extent, shards, -0.22, 0.18)
    return jnp.clip(array, -most, most).astype(held_as)


def setup_inputs(seed: int = 0, part: int = 0) -> dict:
    key_list = jax.random.split(jax.random.key(seed), 5)
    part_keys = jax.random.split(jax.random.fold_in(key_list[4], part), 5)
    return {
        "signal": bell_draw(part_keys[0], (CIN, TW, FIB), 1.0, 6.0, ((2, 16),)),
        "conv_taps": bell_draw(key_list[1], (KS, KS, COUT, CIN), (CIN * KS * KS) ** -0.5, 0.21875),
        "response": bell_draw(key_list[2], (2, COUT, KH), 0.8, 4.0, ((1, 16),), jnp.float32),
        "cotangent": bell_draw(part_keys[3], (COUT, TH, KH), 1.0, 6.0, ((2, 16),)),
    }


inv_root_two = 1.0 / math.sqrt(2.0)
inv_root_tau = 1.0 / math.sqrt(2.0 * math.pi)

def gelu_slope(values):
    return 0.5 * (1.0 + jax.scipy.special.erf(values * inv_root_two)) + values * jnp.exp(-0.5 * values * values) * inv_root_tau

def reference(signal, conv_taps, response, cotangent):
    margin = KS // 2
    padded = jnp.pad(signal, ((0, 0), (margin, margin), (margin, margin)))
    conv_sum = jnp.zeros((COUT, TH * KH), jnp.float32)
    for tap_row in range(KS):
        for tap_col in range(KS):
            patches = padded[:, tap_row:tap_row + 2 * TH:2, tap_col:tap_col + 2 * KH:2].reshape(CIN, TH * KH)
            conv_sum = conv_sum + jnp.dot(conv_taps[tap_row, tap_col], patches, preferred_element_type=jnp.float32)
    conv_out = conv_sum.astype(jnp.bfloat16).reshape(COUT, TH, KH)
    spectra = jnp.fft.fft(conv_out.astype(jnp.float32), axis=-1)
    filter_resp = (response[0] + 1j * response[1])[:, None, :]
    filtered = jnp.real(jnp.fft.ifft(filter_resp * spectra, axis=-1))
    slope_grad = cotangent.astype(jnp.float32) * gelu_slope(filtered)
    grad_spec = jnp.fft.fft(slope_grad, axis=-1)
    cross_spec = spectra * jnp.conj(grad_spec)
    filter_grad = jnp.stack([lax.optimization_barrier(jnp.sum(jnp.real(cross_spec), axis=1)), -lax.optimization_barrier(jnp.sum(jnp.imag(cross_spec), axis=1))]) / KH
    conv_grad = jnp.real(jnp.fft.ifft(jnp.conj(filter_resp) * grad_spec, axis=-1)).astype(jnp.bfloat16)
    grad_flat = conv_grad.reshape(COUT, TH * KH)
    grad_pad = jnp.zeros((CIN, TW + 2 * margin, FIB + 2 * margin), jnp.float32)
    tap_list = []
    for tap_row in range(KS):
        for tap_col in range(KS):
            patches = padded[:, tap_row:tap_row + 2 * TH:2, tap_col:tap_col + 2 * KH:2].reshape(CIN, TH * KH)
            back_term = jnp.dot(conv_taps[tap_row, tap_col].T, grad_flat, preferred_element_type=jnp.float32)
            grad_pad = grad_pad.at[:, tap_row:tap_row + 2 * TH:2, tap_col:tap_col + 2 * KH:2].add(back_term.reshape(CIN, TH, KH))
            tap_list.append(jnp.dot(grad_flat, patches.T, preferred_element_type=jnp.float32))
    input_grad = grad_pad[:, margin:margin + TW, margin:margin + FIB].astype(jnp.bfloat16)
    tap_grad = jnp.stack(tap_list).reshape(KS, KS, COUT, CIN) * (1.0 / math.sqrt(TH * KH))
    return (input_grad, tap_grad, filter_grad)
```

```python
import math

import jax
import jax.numpy as jnp
import numpy as np
from jax import lax
from jax.experimental import pallas as pl
from jax.experimental.pallas import tpu as pltpu
from jax.sharding import PartitionSpec as P

inv_root_two = 1.0 / math.sqrt(2.0)
inv_root_tau = 1.0 / math.sqrt(2.0 * math.pi)
lanes = 128
f32 = jnp.float32
bf16 = jnp.bfloat16
vmem_bytes = 50 * 1024 * 1024


def log2(size):
    bits = size.bit_length() - 1
    assert 1 << bits == size
    return bits


def dot(left, right):
    return jnp.dot(left, right, preferred_element_type=f32)


def one_hot(rows, cols, wanted):
    axis = 0 if wanted.shape[0] == 1 else 1
    index = lax.broadcasted_iota(jnp.int32, (rows, cols), axis)
    return jnp.where(index == wanted, 1.0, 0.0).astype(bf16)


def swap_rows(outer, inner):
    count = outer * inner
    row = lax.broadcasted_iota(jnp.int32, (count, 1), 0)
    source = (row & (inner - 1)) * outer + (row >> log2(inner))
    return one_hot(count, count, source)


def conv_kernel(cin, tw, ks, cout, th, x_ref, w_ref, pp_ref, out_ref, ct_ref):
    width = x_ref.shape[1] - lanes
    half = width // 2
    x2 = dot(swap_rows(tw, cin), x_ref[...]).astype(bf16)
    blank = jnp.zeros((2 * ks * cin, half), bf16)
    pp_ref[0 : 2 * ks * cin, :] = blank
    pp_ref[(tw + 2) * ks * cin : (tw + 4) * ks * cin, :] = blank
    for j in range(ks):
        m = 2 * lax.broadcasted_iota(jnp.int32, (1, half), 1) + (j - 2)
        source = jnp.where(m < 0, width + 2 + m, jnp.where(m >= width, m + 2, m))
        pj = dot(x2, one_hot(width + lanes, half, source)).astype(bf16)
        for s in range(tw):
            at = ((s + 2) * ks + j) * cin
            pp_ref[at : at + cin, :] = pj[s * cin : (s + 1) * cin, :]
    step = 2 * ks * cin
    for t in range(th):
        patches = pp_ref[t * step : t * step + ks * ks * cin, :]
        ct_ref[t * cout : (t + 1) * cout, :] = dot(w_ref[...], patches).astype(bf16)
    out_ref[...] = dot(swap_rows(cout, th), ct_ref[...]).astype(bf16)


def split(values):
    high = values.astype(bf16)
    return high, (values - high.astype(f32)).astype(bf16)


def dot_split(left, right):
    return dot(left[0], right[0]) + (dot(left[0], right[1]) + dot(left[1], right[0]))


def filter_kernel(
    chans, th, rv_ref, re_ref, im_ref, o1_ref, o1b_ref, i2_ref, i2b_ref, tc_ref, ts_ref, fg_ref, out_ref
):
    blocks = rv_ref.shape[0]
    per = rv_ref.shape[2] // lanes
    outer = blocks * per
    rows = outer * th
    waves = outer * lanes
    o1 = (o1_ref[0], o1_ref[1])
    o1b = (o1b_ref[0], o1b_ref[1])
    i2 = (i2_ref[0], i2_ref[1])
    i2b = (i2b_ref[0], i2b_ref[1])
    tcos = tc_ref[...]
    tsin = ts_ref[...]

    def gathered(first):
        cols = []
        whole = [rv_ref[d].astype(f32) for d in range(blocks)]
        for c in range(chans):
            tiles = []
            for d in range(blocks):
                at = first + c * th
                for h in range(per):
                    tiles.append(whole[d][at : at + th, h * lanes : (h + 1) * lanes])
            cols.append(jnp.concatenate(tiles, axis=0))
        return jnp.concatenate(cols, axis=1)

    def forward(first):
        wide = []
        for c in range(chans):
            fr = first[:rows, c * lanes : (c + 1) * lanes]
            fi = first[rows:, c * lanes : (c + 1) * lanes]
            wide.append(jnp.concatenate([fr * tcos + fi * tsin, fi * tcos - fr * tsin], axis=1))
        spec = dot_split(split(jnp.concatenate(wide, axis=0)), i2)
        return spec[:, :lanes], spec[:, lanes:]

    def backward(sr, si):
        back = dot_split(split(jnp.concatenate([sr, si], axis=1)), i2b)
        cols = []
        for c in range(chans):
            br = back[c * rows : (c + 1) * rows, :lanes]
            bi = back[c * rows : (c + 1) * rows, lanes:]
            cols.append(jnp.concatenate([br * tcos - bi * tsin, bi * tcos + br * tsin], axis=0))
        return dot_split(o1b, split(jnp.concatenate(cols, axis=1))) * (1.0 / waves)

    def spread(ref):
        flat = ref[...]
        return jnp.broadcast_to(flat[:, None, :], (flat.shape[0], th, lanes)).reshape(
            flat.shape[0] * th, lanes
        )

    resp_r = spread(re_ref)
    resp_i = spread(im_ref)
    x = gathered(0).astype(bf16)
    sr, si = forward(dot(o1[0], x) + dot(o1[1], x))
    v = backward(resp_r * sr - resp_i * si, resp_r * si + resp_i * sr)
    slope = 0.5 * (1.0 + lax.erf(v * inv_root_two)) + v * jnp.exp(-0.5 * v * v) * inv_root_tau
    g = gathered(chans * th) * slope
    gr, gi = forward(dot_split(o1, split(g)))
    scale = 1.0 / waves
    fg_ref[0] = jnp.sum((sr * gr + si * gi).reshape(chans * outer, th, lanes), axis=1) * scale
    fg_ref[1] = jnp.sum((sr * gi - si * gr).reshape(chans * outer, th, lanes), axis=1) * scale
    y = backward(resp_r * gr + resp_i * gi, resp_r * gi - resp_i * gr)
    lane = lax.broadcasted_iota(jnp.int32, (th, lanes), 1)
    zero = jnp.zeros((th, lanes), f32)
    for d in range(blocks):
        parts = []
        for c in range(chans):
            col = y[:, c * lanes : (c + 1) * lanes]
            low = col[(d * per - 1) * th : d * per * th] if d > 0 else zero
            high = col[(d + 1) * per * th : ((d + 1) * per + 1) * th] if d < blocks - 1 else zero
            rim = jnp.where(lane == lanes - 1, low, jnp.where(lane == 0, high, 0.0))
            tiles = [col[(d * per + h) * th : (d * per + h + 1) * th] for h in range(per)]
            parts.append(jnp.concatenate(tiles + [rim], axis=1))
        out_ref[d] = jnp.concatenate(parts, axis=0).astype(bf16)


def taps_kernel(cin, ks, cout, th, g_ref, pp_ref, gt_ref, tap_ref):
    half = pp_ref.shape[1]
    gt_ref[...] = dot(swap_rows(th, cout), g_ref[...]).astype(bf16)
    step = 2 * ks * cin
    total = None
    for t in range(th):
        term = lax.dot_general(
            gt_ref[t * cout : (t + 1) * cout, :half],
            pp_ref[t * step : t * step + ks * ks * cin, :],
            (((1,), (1,)), ((), ())),
            preferred_element_type=f32,
        )
        total = term if total is None else total + term
    tap_ref[...] = total


def input_kernel(cin, tw, cout, th, gt_ref, v_ref, out_ref, gg_ref, xo_ref):
    ext = gt_ref.shape[1]
    half = ext - lanes
    blank = jnp.zeros((3 * cout, half), bf16)
    gg_ref[0 : 3 * cout, :] = blank
    gg_ref[(th + 1) * 3 * cout : (th + 2) * 3 * cout, :] = blank
    p = lax.broadcasted_iota(jnp.int32, (1, half), 1)
    g2 = gt_ref[...]
    for sh in range(3):
        if sh == 1:
            moved = g2[:, :half]
        else:
            source = p + 1 if sh == 0 else jnp.where(p == 0, ext - 1, p - 1)
            moved = dot(g2, one_hot(ext, half, source)).astype(bf16)
        for t in range(th):
            at = ((t + 1) * 3 + sh) * cout
            gg_ref[at : at + cout, :] = moved[t * cout : (t + 1) * cout, :]
    for q in range(th):
        dx = dot(v_ref[...], gg_ref[q * 3 * cout : (q + 3) * 3 * cout, :]).astype(bf16)
        for ps in range(2):
            for pm in range(2):
                at = (ps * 2 + pm) * cin
                row = (2 * q + ps) * cin
                xo_ref[row : row + cin, pm * half : (pm + 1) * half] = dx[at : at + cin, :]
    m = lax.broadcasted_iota(jnp.int32, (1, 2 * half), 1)
    weave = one_hot(2 * half, 2 * half, (m & 1) * half + (m >> 1))
    woven = dot(xo_ref[...], weave).astype(bf16)
    out_ref[...] = dot(swap_rows(cin, tw), woven).astype(bf16)


def dft_tables(outer, th):
    waves = outer * lanes
    turn = 2.0 * math.pi
    a = np.arange(outer)
    b = np.arange(lanes)
    ang = turn * ((a[:, None] * a[None, :]) % outer) / outer
    eye = np.eye(th)
    o1 = np.concatenate([np.kron(np.cos(ang), eye), -np.kron(np.sin(ang), eye)], axis=0)
    ang = turn * ((b[:, None] * b[None, :]) % lanes) / lanes
    i2 = np.block([[np.cos(ang), -np.sin(ang)], [np.sin(ang), np.cos(ang)]])
    ang = np.repeat(turn * (a[:, None] * b[None, :]) / waves, th, axis=0)

    def halves(table):
        table = table.astype(np.float32)
        high = table.astype(bf16)
        return np.stack([high, (table - high.astype(np.float32)).astype(bf16)])

    return (
        halves(o1),
        halves(o1.T),
        halves(i2),
        halves(i2.T),
        np.cos(ang).astype(np.float32),
        np.sin(ang).astype(np.float32),
    )


def call(body, out_shape, scratch=(), flops=0):
    many = isinstance(out_shape, (list, tuple))
    return pl.pallas_call(
        body,
        out_shape=out_shape,
        out_specs=[pl.BlockSpec(memory_space=pltpu.VMEM)] * len(out_shape)
        if many
        else pl.BlockSpec(memory_space=pltpu.VMEM),
        scratch_shapes=list(scratch),
        compiler_params=pltpu.CompilerParams(vmem_limit_bytes=vmem_bytes),
        cost_estimate=pl.CostEstimate(flops=flops, bytes_accessed=4000000, transcendentals=0),
    )


def phase_weights(conv_taps):
    ks, _, cout, cin = conv_taps.shape
    none = jnp.zeros((cin, cout), conv_taps.dtype)
    turned = conv_taps.transpose(0, 1, 3, 2)
    rows = []
    for ps in range(2):
        for pm in range(2):
            cols = []
            for ti in range(3):
                i = 4 - 2 * ti + ps
                for sh in range(3):
                    j = 2 * sh + pm
                    if ps:
                        i = (None, 3, 1)[ti]
                    inside = i is not None and i < ks and j < ks
                    cols.append(turned[i, j] if inside else none)
            rows.append(jnp.concatenate(cols, axis=1))
    return jnp.concatenate(rows, axis=0)


def per_device(signal, conv_taps, response, cotangent):
    ks, _, cout, cin = conv_taps.shape
    tw, width = signal.shape[1:]
    th, half = cotangent.shape[1:]
    count = lax.axis_size("fibre")
    chans = response.shape[1]
    waves = response.shape[2]
    outer = waves // lanes
    shape = jax.ShapeDtypeStruct

    up = [(i, i + 1) for i in range(count - 1)]
    down = [(b, a) for a, b in up]
    low = lax.ppermute(signal[:, :, width - 2 :], "fibre", up)
    high = lax.ppermute(signal[:, :, :2], "fibre", down)
    rim = jnp.pad(jnp.concatenate([low, high], axis=2), ((0, 0), (0, 0), (0, lanes - 4)))
    ext = jnp.concatenate([signal, rim], axis=2).reshape(cin * tw, width + lanes)
    taps_flat = conv_taps.transpose(2, 0, 1, 3).reshape(cout, ks * ks * cin)
    weights = phase_weights(conv_taps)
    tables = dft_tables(outer, th)
    arranged = response.reshape(2, chans, lanes, outer).transpose(0, 1, 3, 2)
    arranged = arranged.reshape(2, chans * outer, lanes)

    def conv_body(*refs):
        conv_kernel(cin, tw, ks, cout, th, *refs)

    patches, conv_out = call(
        conv_body,
        [shape(((tw + 4) * ks * cin, half), bf16), shape((cout * th, half), bf16)],
        [pltpu.VMEM((cout * th, half), bf16)],
    )(ext, taps_flat)

    group = chans * th
    sent = jnp.concatenate(
        [conv_out.reshape(count, group, half), cotangent.reshape(count, group, half)], axis=1
    )
    got = lax.all_to_all(sent, "fibre", split_axis=0, concat_axis=0, tiled=True)

    def filter_body(*refs):
        filter_kernel(chans, th, *refs)

    fgrad, blocks = call(
        filter_body,
        [shape((2, chans * outer, lanes), f32), shape((count, group, half + lanes), bf16)],
    )(got, arranged[0], arranged[1], *tables)
    filter_grad = (
        fgrad.reshape(2, chans, outer, lanes).transpose(0, 1, 3, 2).reshape(2, chans, waves)
    )
    grads = lax.all_to_all(blocks, "fibre", split_axis=0, concat_axis=0, tiled=True)
    grads = grads.reshape(cout * th, half + lanes)

    def taps_body(*refs):
        taps_kernel(cin, ks, cout, th, *refs)

    turned, local_taps = call(
        taps_body,
        [shape((cout * th, half + lanes), bf16), shape((cout, ks * ks * cin), f32)],
    )(grads, patches)
    share = cout * ks * ks * cin // count
    terms = lax.all_to_all(
        local_taps.reshape(count, 8, share // 8), "fibre", split_axis=0, concat_axis=0, tiled=True
    )

    def input_body(*refs):
        input_kernel(cin, tw, cout, th, *refs)

    input_grad = call(
        input_body,
        shape((cin * tw, width), bf16),
        [pltpu.VMEM(((th + 2) * 3 * cout, half), bf16), pltpu.VMEM((cin * tw, width), bf16)],
        flops=1500000000,
    )(turned, weights)

    part = jnp.sum(terms, axis=0) * (1.0 / math.sqrt(th * waves))
    all_taps = lax.all_to_all(
        jnp.broadcast_to(part[None], (count, 8, share // 8)),
        "fibre",
        split_axis=0,
        concat_axis=0,
        tiled=True,
    )
    tap_grad = all_taps.reshape(cout, ks, ks, cin).transpose(1, 2, 0, 3)
    return (input_grad.reshape(signal.shape), tap_grad, filter_grad)


def solution(mesh):
    in_specs = (P("parts", None, "fibre"), P(), P(None, "fibre", None), P("parts", None, "fibre"))
    out_specs = (P("parts", None, "fibre"), P("parts", None, None, None), P("parts", "fibre", None))
    return jax.shard_map(
        per_device, mesh=mesh, in_specs=in_specs, out_specs=out_specs, check_vma=False
    )
```

```python
import math

import jax
import jax.numpy as jnp
import numpy as np
from jax import lax
from jax.experimental import pallas as pl
from jax.experimental.pallas import tpu as pltpu
from jax.sharding import PartitionSpec as P

inv_root_two = 1.0 / math.sqrt(2.0)
inv_root_tau = 1.0 / math.sqrt(2.0 * math.pi)
lanes = 128
f32 = jnp.float32
bf16 = jnp.bfloat16
vmem_bytes = 50 * 1024 * 1024


def log2(size):
    bits = size.bit_length() - 1
    assert 1 << bits == size
    return bits


def dot(left, right):
    return jnp.dot(left, right, preferred_element_type=f32)


def one_hot(rows, cols, wanted):
    axis = 0 if wanted.shape[0] == 1 else 1
    index = lax.broadcasted_iota(jnp.int32, (rows, cols), axis)
    return jnp.where(index == wanted, 1.0, 0.0).astype(bf16)


def swap_rows(outer, inner):
    count = outer * inner
    row = lax.broadcasted_iota(jnp.int32, (count, 1), 0)
    source = (row & (inner - 1)) * outer + (row >> log2(inner))
    return one_hot(count, count, source)


def split(values):
    high = values.astype(bf16)
    return high, (values - high.astype(f32)).astype(bf16)


def dot_split(left, right):
    return dot(left[0], right[0]) + (dot(left[0], right[1]) + dot(left[1], right[0]))


def dft_tables(outer, th):
    waves = outer * lanes
    turn = 2.0 * math.pi
    a = np.arange(outer)
    b = np.arange(lanes)
    ang = turn * ((a[:, None] * a[None, :]) % outer) / outer
    eye = np.eye(th)
    o1 = np.concatenate([np.kron(np.cos(ang), eye), -np.kron(np.sin(ang), eye)], axis=0)
    ang = turn * ((b[:, None] * b[None, :]) % lanes) / lanes
    i2 = np.block([[np.cos(ang), -np.sin(ang)], [np.sin(ang), np.cos(ang)]])
    ang = np.repeat(turn * (a[:, None] * b[None, :]) / waves, th, axis=0)

    def halves(table):
        table = table.astype(np.float32)
        high = table.astype(bf16)
        return np.stack([high, (table - high.astype(np.float32)).astype(bf16)])

    return (
        halves(o1),
        halves(o1.T),
        halves(i2),
        halves(i2.T),
        np.cos(ang).astype(np.float32),
        np.sin(ang).astype(np.float32),
    )


MESH = pl.DeviceIdType.MESH


def section_kernel(dims, *refs):
    (cin, tw, ks, cout, th, chans, count, cuts) = dims
    (x_ref, cot_ref, w_ref, v_ref, re_ref, im_ref) = refs[:6]
    table_refs = refs[6:12]
    (dx_ref, fg_ref, tap_ref) = refs[12:15]
    (o1_ref, o1b_ref, i2_ref, i2b_ref, tc_ref, ts_ref) = held = refs[15:21]
    (lo_ref, hi_ref, pp_ref, ct_ref, sent_ref, gotx_ref, gotc_ref) = refs[21:28]
    (back_ref, grad_ref, gt_ref, gg_ref, xo_ref, part_ref, term_ref, whole_ref) = refs[28:36]
    (table_sem, halo_send, halo_recv, c_send, c_recv, x_send, x_recv) = refs[36:43]
    (g_send, g_recv, t_send, t_recv, w_send, w_recv) = refs[43:49]
    me = lax.axis_index("fibre")
    width = x_ref.shape[1]
    half = width // 2
    per = half // lanes
    outer = count * per
    rows = outer * th
    waves = outer * lanes
    group = chans * th

    def peer_of(k):
        return lax.rem(me + k, count)

    barrier = pltpu.get_barrier_semaphore()

    def greet(k, carry):
        pl.semaphore_signal(
            barrier, inc=1, device_id={"fibre": peer_of(k)}, device_id_type=MESH
        )
        return carry

    lax.fori_loop(1, count, greet, 0)
    loads = [
        pltpu.make_async_copy(src, dst, table_sem.at[i])
        for i, (src, dst) in enumerate(zip(table_refs, held))
    ]
    for load in loads:
        load.start()
    pl.semaphore_wait(barrier, count - 1)

    def remote(src, dst, ssem, rsem, peer):
        return pltpu.make_async_remote_copy(
            src_ref=src,
            dst_ref=dst,
            send_sem=ssem,
            recv_sem=rsem,
            device_id={"fibre": peer},
            device_id_type=MESH,
        )

    def exchange(src, dst, ssem, rsem):
        def copy(k):
            peer = peer_of(k)
            return remote(src.at[peer], dst.at[me], ssem.at[k], rsem.at[k], peer)

        def go(k, carry):
            copy(k).start()
            return carry

        def end(k, carry):
            copy(k).wait()
            return carry

        lax.fori_loop(1, count, go, 0)
        return lambda: lax.fori_loop(1, count, end, 0)

    to_right = remote(
        x_ref.at[:, width - lanes : width], lo_ref, halo_send.at[0], halo_recv.at[0], peer_of(1)
    )
    to_left = remote(
        x_ref.at[:, 0:lanes], hi_ref, halo_send.at[1], halo_recv.at[1], peer_of(count - 1)
    )
    to_right.start()
    to_left.start()
    end_cot = exchange(cot_ref, gotc_ref, c_send, c_recv)
    gotc_ref[me] = cot_ref[me]

    order = swap_rows(tw, cin)
    x2 = dot(order, x_ref[...]).astype(bf16)
    blank = jnp.zeros((2 * ks * cin, half), bf16)
    pp_ref[0 : 2 * ks * cin, :] = blank
    pp_ref[(tw + 2) * ks * cin : (tw + 4) * ks * cin, :] = blank
    to_right.wait()
    to_left.wait()
    lo2 = dot(order, lo_ref[...]).astype(bf16)
    hi2 = dot(order, hi_ref[...]).astype(bf16)
    for j in range(ks):
        m = 2 * lax.broadcasted_iota(jnp.int32, (1, half), 1) + (j - 2)
        pj = dot(x2, one_hot(width, half, m))
        if j < 2:
            pj += dot(lo2, one_hot(lanes, half, jnp.where((m < 0) & (me > 0), lanes + m, -1)))
        if j > 3:
            inside = (m >= width) & (me < count - 1)
            pj += dot(hi2, one_hot(lanes, half, jnp.where(inside, m - width, -1)))
        pj = pj.astype(bf16)
        for s in range(tw):
            at = ((s + 2) * ks + j) * cin
            pp_ref[at : at + cin, :] = pj[s * cin : (s + 1) * cin, :]
    step = 2 * ks * cin
    taps_rows = ks * ks * cin
    for t in range(th):
        patches = pp_ref[t * step : t * step + taps_rows, :]
        ct_ref[t * cout : (t + 1) * cout, :] = dot(w_ref[...], patches).astype(bf16)
    conv_out = dot(swap_rows(cout, th), ct_ref[...]).astype(bf16)
    sent_ref[...] = conv_out.reshape(count, group, half)
    end_conv = exchange(sent_ref, gotx_ref, x_send, x_recv)
    gotx_ref[me] = sent_ref[me]
    for load in loads:
        load.wait()
    end_cot()

    o1 = (o1_ref[0], o1_ref[1])
    o1b = (o1b_ref[0], o1b_ref[1])
    i2 = (i2_ref[0], i2_ref[1])
    i2b = (i2b_ref[0], i2b_ref[1])
    tcos = tc_ref[...]
    tsin = ts_ref[...]

    def gathered(ref):
        cols = []
        whole = [ref[d].astype(f32) for d in range(count)]
        for c in range(chans):
            tiles = []
            for d in range(count):
                at = c * th
                for h in range(per):
                    tiles.append(whole[d][at : at + th, h * lanes : (h + 1) * lanes])
            cols.append(jnp.concatenate(tiles, axis=0))
        return jnp.concatenate(cols, axis=1)

    def forward(first):
        wide = []
        for c in range(chans):
            fr = first[:rows, c * lanes : (c + 1) * lanes]
            fi = first[rows:, c * lanes : (c + 1) * lanes]
            wide.append(jnp.concatenate([fr * tcos + fi * tsin, fi * tcos - fr * tsin], axis=1))
        spec = dot_split(split(jnp.concatenate(wide, axis=0)), i2)
        return spec[:, :lanes], spec[:, lanes:]

    def backward(sr, si):
        back = dot_split(split(jnp.concatenate([sr, si], axis=1)), i2b)
        cols = []
        for c in range(chans):
            br = back[c * rows : (c + 1) * rows, :lanes]
            bi = back[c * rows : (c + 1) * rows, lanes:]
            cols.append(jnp.concatenate([br * tcos - bi * tsin, bi * tcos + br * tsin], axis=0))
        return dot_split(o1b, split(jnp.concatenate(cols, axis=1))) * (1.0 / waves)

    def spread(ref):
        flat = ref[...]
        return jnp.broadcast_to(flat[:, None, :], (flat.shape[0], th, lanes)).reshape(
            flat.shape[0] * th, lanes
        )

    resp_r = spread(re_ref)
    resp_i = spread(im_ref)
    end_conv()
    x = gathered(gotx_ref).astype(bf16)
    sr, si = forward(dot(o1[0], x) + dot(o1[1], x))
    v = backward(resp_r * sr - resp_i * si, resp_r * si + resp_i * sr)
    slope = 0.5 * (1.0 + lax.erf(v * inv_root_two)) + v * jnp.exp(-0.5 * v * v) * inv_root_tau
    g = gathered(gotc_ref) * slope
    gr, gi = forward(dot_split(o1, split(g)))
    scale = 1.0 / waves
    fg_ref[0] = jnp.sum((sr * gr + si * gi).reshape(chans * outer, th, lanes), axis=1) * scale
    fg_ref[1] = jnp.sum((sr * gi - si * gr).reshape(chans * outer, th, lanes), axis=1) * scale
    y = backward(resp_r * gr + resp_i * gi, resp_r * gi - resp_i * gr)
    lane = lax.broadcasted_iota(jnp.int32, (th, lanes), 1)
    zero = jnp.zeros((th, lanes), f32)
    for d in range(count):
        parts = []
        for c in range(chans):
            col = y[:, c * lanes : (c + 1) * lanes]
            low = col[(d * per - 1) * th : d * per * th] if d > 0 else zero
            high = col[(d + 1) * per * th : ((d + 1) * per + 1) * th] if d < count - 1 else zero
            rim = jnp.where(lane == lanes - 1, low, jnp.where(lane == 0, high, 0.0))
            tiles = [col[(d * per + h) * th : (d * per + h + 1) * th] for h in range(per)]
            parts.append(jnp.concatenate(tiles + [rim], axis=1))
        back_ref[d] = jnp.concatenate(parts, axis=0).astype(bf16)
    end_grad = exchange(back_ref, grad_ref, g_send, g_recv)
    grad_ref[me] = back_ref[me]
    end_grad()

    ext = half + lanes
    g_all = grad_ref[...].reshape(cout * th, ext)
    gt_ref[...] = dot(swap_rows(th, cout), g_all).astype(bf16)
    total = None
    for t in range(th):
        term = lax.dot_general(
            gt_ref[t * cout : (t + 1) * cout, :half],
            pp_ref[t * step : t * step + taps_rows, :],
            (((1,), (1,)), ((), ())),
            preferred_element_type=f32,
        )
        total = term if total is None else total + term
    part_width = part_ref.shape[2]
    total = jnp.concatenate(
        [total, jnp.zeros((cout, cuts * part_width - taps_rows), f32)], axis=1
    )
    for r in range(cout // 8):
        for p in range(cuts):
            part_ref[r * cuts + p] = total[
                r * 8 : (r + 1) * 8, p * part_width : (p + 1) * part_width
            ]
    end_terms = exchange(part_ref, term_ref, t_send, t_recv)
    term_ref[me] = part_ref[me]

    blank = jnp.zeros((3 * cout, half), bf16)
    gg_ref[0 : 3 * cout, :] = blank
    gg_ref[(th + 1) * 3 * cout : (th + 2) * 3 * cout, :] = blank
    p = lax.broadcasted_iota(jnp.int32, (1, half), 1)
    g2 = gt_ref[...]
    for sh in range(3):
        if sh == 1:
            moved = g2[:, :half]
        else:
            source = p + 1 if sh == 0 else jnp.where(p == 0, ext - 1, p - 1)
            moved = dot(g2, one_hot(ext, half, source)).astype(bf16)
        for t in range(th):
            at = ((t + 1) * 3 + sh) * cout
            gg_ref[at : at + cout, :] = moved[t * cout : (t + 1) * cout, :]

    end_terms()
    whole_ref[me] = jnp.sum(term_ref[...], axis=0) * (1.0 / math.sqrt(th * waves))

    def share(k):
        return remote(whole_ref.at[me], whole_ref.at[me], w_send.at[k], w_recv.at[k], peer_of(k))

    def share_start(k, carry):
        share(k).start()
        return carry

    def share_end(k, carry):
        share(k).wait()
        return carry

    lax.fori_loop(1, count, share_start, 0)

    for q in range(th):
        dx = lax.dot_general(
            v_ref[...],
            gg_ref[q * 3 * cout : (q + 3) * 3 * cout, :],
            (((0,), (0,)), ((), ())),
            preferred_element_type=f32,
        ).astype(bf16)
        for ps in range(2):
            for pm in range(2):
                at = (ps * 2 + pm) * cin
                row = (2 * q + ps) * cin
                xo_ref[row : row + cin, pm * half : (pm + 1) * half] = dx[at : at + cin, :]
    m = lax.broadcasted_iota(jnp.int32, (1, width), 1)
    weave = one_hot(width, width, (m & 1) * half + (m >> 1))
    woven = dot(xo_ref[...], weave).astype(bf16)
    dx_ref[...] = dot(swap_rows(cin, tw), woven).astype(bf16)
    lax.fori_loop(1, count, share_end, 0)
    tap_ref[...] = whole_ref[...]


def phase_weights(conv_taps):
    ks, _, cout, cin = conv_taps.shape
    none = jnp.zeros((cout, cin), conv_taps.dtype)
    cols = []
    for ps in range(2):
        for pm in range(2):
            rows = []
            for ti in range(3):
                i = (None, 3, 1)[ti] if ps else 4 - 2 * ti
                for sh in range(3):
                    j = 2 * sh + pm
                    rows.append(conv_taps[i, j] if i is not None and j < ks else none)
            cols.append(jnp.concatenate(rows, axis=0))
    return jnp.concatenate(cols, axis=1)


def per_device(signal, conv_taps, response, cotangent):
    ks, _, cout, cin = conv_taps.shape
    tw, width = signal.shape[1:]
    th, half = cotangent.shape[1:]
    count = lax.axis_size("fibre")
    chans = response.shape[1]
    waves = response.shape[2]
    outer = waves // lanes
    group = chans * th
    taps_rows = ks * ks * cin
    parts = count * 8 // cout
    assert parts * cout == count * 8
    part_width = -(-taps_rows // (parts * lanes)) * lanes
    shape = jax.ShapeDtypeStruct
    taps_flat = conv_taps.transpose(2, 0, 1, 3).reshape(cout, taps_rows)
    tables = dft_tables(outer, th)
    arranged = response.reshape(2, chans, lanes, outer).transpose(0, 1, 3, 2)
    arranged = arranged.reshape(2, chans * outer, lanes)
    dims = (cin, tw, ks, cout, th, chans, count, parts)

    def body(*refs):
        section_kernel(dims, *refs)

    vmem = pl.BlockSpec(memory_space=pltpu.VMEM)
    every = pltpu.SemaphoreType.DMA((count,))
    ext = half + lanes
    dx, fgrad, taps = pl.pallas_call(
        body,
        out_shape=[
            shape((cin * tw, width), bf16),
            shape((2, chans * outer, lanes), f32),
            shape((count, 8, part_width), f32),
        ],
        in_specs=[vmem] * 6 + [pl.BlockSpec(memory_space=pl.ANY)] * 6,
        out_specs=[vmem] * 3,
        scratch_shapes=[pltpu.VMEM(table.shape, table.dtype) for table in tables]
        + [
            pltpu.VMEM((cin * tw, lanes), bf16),
            pltpu.VMEM((cin * tw, lanes), bf16),
            pltpu.VMEM(((tw + 4) * ks * cin, half), bf16),
            pltpu.VMEM((cout * th, half), bf16),
            pltpu.VMEM((count, group, half), bf16),
            pltpu.VMEM((count, group, half), bf16),
            pltpu.VMEM((count, group, half), bf16),
            pltpu.VMEM((count, group, ext), bf16),
            pltpu.VMEM((count, group, ext), bf16),
            pltpu.VMEM((cout * th, ext), bf16),
            pltpu.VMEM(((th + 2) * 3 * cout, half), bf16),
            pltpu.VMEM((cin * tw, width), bf16),
            pltpu.VMEM((count, 8, part_width), f32),
            pltpu.VMEM((count, 8, part_width), f32),
            pltpu.VMEM((count, 8, part_width), f32),
            pltpu.SemaphoreType.DMA((6,)),
            pltpu.SemaphoreType.DMA((2,)),
            pltpu.SemaphoreType.DMA((2,)),
        ]
        + [every] * 10,
        compiler_params=pltpu.CompilerParams(
            vmem_limit_bytes=vmem_bytes, collective_id=0, has_side_effects=True
        ),
        cost_estimate=pl.CostEstimate(
            flops=6000000000, bytes_accessed=8000000, transcendentals=0
        ),
    )(
        signal.reshape(cin * tw, width),
        cotangent.reshape(count, group, half),
        taps_flat,
        phase_weights(conv_taps),
        arranged[0],
        arranged[1],
        *tables,
    )
    filter_grad = (
        fgrad.reshape(2, chans, outer, lanes).transpose(0, 1, 3, 2).reshape(2, chans, waves)
    )
    tap_grad = (
        taps.reshape(cout // 8, parts, 8, part_width)
        .transpose(0, 2, 1, 3)
        .reshape(cout, parts * part_width)[:, :taps_rows]
        .reshape(cout, ks, ks, cin)
        .transpose(1, 2, 0, 3)
    )
    return (dx.reshape(signal.shape), tap_grad, filter_grad)


def solution(mesh):
    in_specs = (P("parts", None, "fibre"), P(), P(None, "fibre", None), P("parts", None, "fibre"))
    out_specs = (P("parts", None, "fibre"), P("parts", None, None, None), P("parts", "fibre", None))
    return jax.shard_map(
        per_device, mesh=mesh, in_specs=in_specs, out_specs=out_specs, check_vma=False
    )
```

```python
import math

import jax
import jax.numpy as jnp
import numpy as np
from jax import lax
from jax.experimental import pallas as pl
from jax.experimental.pallas import tpu as pltpu
from jax.sharding import PartitionSpec as P

inv_root_two = 1.0 / math.sqrt(2.0)
inv_root_tau = 1.0 / math.sqrt(2.0 * math.pi)
lanes = 128
f32 = jnp.float32
bf16 = jnp.bfloat16
vmem_bytes = 50 * 1024 * 1024


def log2(size):
    bits = size.bit_length() - 1
    assert 1 << bits == size
    return bits


def dot(left, right):
    return jnp.dot(left, right, preferred_element_type=f32)


def one_hot(rows, cols, wanted):
    axis = 0 if wanted.shape[0] == 1 else 1
    index = lax.broadcasted_iota(jnp.int32, (rows, cols), axis)
    return jnp.where(index == wanted, 1.0, 0.0).astype(bf16)


def swap_rows(outer, inner):
    count = outer * inner
    row = lax.broadcasted_iota(jnp.int32, (count, 1), 0)
    source = (row & (inner - 1)) * outer + (row >> log2(inner))
    return one_hot(count, count, source)


def split(values):
    high = values.astype(bf16)
    return high, (values - high.astype(f32)).astype(bf16)


def dot_split(left, right):
    return dot(left[0], right[0]) + (dot(left[0], right[1]) + dot(left[1], right[0]))


def dft_tables(outer, th):
    waves = outer * lanes
    turn = 2.0 * math.pi
    a = np.arange(outer)
    b = np.arange(lanes)
    ang = turn * ((a[:, None] * a[None, :]) % outer) / outer
    eye = np.eye(th)
    o1 = np.concatenate([np.kron(np.cos(ang), eye), -np.kron(np.sin(ang), eye)], axis=0)
    ang = turn * ((b[:, None] * b[None, :]) % lanes) / lanes
    i2 = np.block([[np.cos(ang), -np.sin(ang)], [np.sin(ang), np.cos(ang)]])
    ang = np.repeat(turn * (a[:, None] * b[None, :]) / waves, th, axis=0)

    def halves(table):
        table = table.astype(np.float32)
        high = table.astype(bf16)
        return np.stack([high, (table - high.astype(np.float32)).astype(bf16)])

    return (
        halves(o1),
        halves(o1.T),
        halves(i2),
        halves(i2.T),
        np.cos(ang).astype(np.float32),
        np.sin(ang).astype(np.float32),
    )


MESH = pl.DeviceIdType.MESH


def section_kernel(dims, *refs):
    (cin, tw, ks, cout, th, chans, count, cuts) = dims
    (x_ref, cot_ref, w_ref, resp_ref) = refs[:4]
    table_refs = refs[4:10]
    (dx_ref, fg_ref, tap_ref) = refs[10:13]
    (o1_ref, o1b_ref, i2_ref, i2b_ref, tc_ref, ts_ref) = held = refs[13:19]
    (lo_ref, hi_ref, pp_ref, ct_ref, sent_ref, gotx_ref, gotc_ref) = refs[19:26]
    (back_ref, grad_ref, gt_ref, gg_ref, xo_ref, part_ref, term_ref, whole_ref) = refs[26:34]
    (glo_ref, ghi_ref, v_ref) = refs[34:37]
    (table_sem, halo_send, halo_recv, c_send, c_recv, x_send, x_recv) = refs[37:44]
    (g_send, g_recv, t_send, t_recv, w_send, w_recv) = refs[44:50]
    me = lax.axis_index("fibre")
    width = x_ref.shape[1]
    half = width // 2
    per = half // lanes
    outer = count * per
    rows = outer * th
    waves = outer * lanes
    group = chans * th

    def peer_of(k):
        return lax.rem(me + k, count)

    barrier = pltpu.get_barrier_semaphore()

    def greet(k, carry):
        pl.semaphore_signal(
            barrier, inc=1, device_id={"fibre": peer_of(k)}, device_id_type=MESH
        )
        return carry

    lax.fori_loop(1, count, greet, 0)
    loads = [
        pltpu.make_async_copy(src, dst, table_sem.at[i])
        for i, (src, dst) in enumerate(zip(table_refs, held))
    ]
    for load in loads:
        load.start()
    pl.semaphore_wait(barrier, count - 1)

    def remote(src, dst, ssem, rsem, peer):
        return pltpu.make_async_remote_copy(
            src_ref=src,
            dst_ref=dst,
            send_sem=ssem,
            recv_sem=rsem,
            device_id={"fibre": peer},
            device_id_type=MESH,
        )

    def exchange(src, dst, ssem, rsem, last=count):
        def copy(k):
            peer = peer_of(k)
            return remote(src.at[peer], dst.at[me], ssem.at[k], rsem.at[k], peer)

        def go(k, carry):
            copy(k).start()
            return carry

        def end(k, carry):
            copy(k).wait()
            return carry

        lax.fori_loop(1, last, go, 0)
        rest = lambda: lax.fori_loop(last, count, go, 0)
        finish = lambda: lax.fori_loop(1, count, end, 0)
        return (rest, finish) if last < count else finish

    to_right = remote(
        x_ref.at[:, width - lanes : width], lo_ref, halo_send.at[0], halo_recv.at[0], peer_of(1)
    )
    to_left = remote(
        x_ref.at[:, 0:lanes], hi_ref, halo_send.at[1], halo_recv.at[1], peer_of(count - 1)
    )
    to_right.start()
    to_left.start()
    more_cot, end_cot = exchange(cot_ref, gotc_ref, c_send, c_recv, count // 2)
    gotc_ref[me] = cot_ref[me]

    order = swap_rows(tw, cin)
    x2 = dot(order, x_ref[...]).astype(bf16)
    blank = jnp.zeros((2 * ks * cin, half), bf16)
    pp_ref[0 : 2 * ks * cin, :] = blank
    pp_ref[(tw + 2) * ks * cin : (tw + 4) * ks * cin, :] = blank
    to_right.wait()
    to_left.wait()
    lo2 = dot(order, lo_ref[...]).astype(bf16)
    hi2 = dot(order, hi_ref[...]).astype(bf16)
    for j in range(ks):
        m = 2 * lax.broadcasted_iota(jnp.int32, (1, half), 1) + (j - 2)
        pj = dot(x2, one_hot(width, half, m))
        if j < 2:
            pj += dot(lo2, one_hot(lanes, half, jnp.where((m < 0) & (me > 0), lanes + m, -1)))
        if j > 3:
            inside = (m >= width) & (me < count - 1)
            pj += dot(hi2, one_hot(lanes, half, jnp.where(inside, m - width, -1)))
        pj = pj.astype(bf16)
        for s in range(tw):
            at = ((s + 2) * ks + j) * cin
            pp_ref[at : at + cin, :] = pj[s * cin : (s + 1) * cin, :]
    step = 2 * ks * cin
    taps_rows = ks * ks * cin
    for t in range(th):
        patches = pp_ref[t * step : t * step + taps_rows, :]
        ct_ref[t * cout : (t + 1) * cout, :] = lax.dot_general(
            w_ref[...], patches, (((0,), (0,)), ((), ())), preferred_element_type=f32
        ).astype(bf16)
    conv_out = dot(swap_rows(cout, th), ct_ref[...]).astype(bf16)
    sent_ref[...] = conv_out.reshape(count, group, half)
    end_conv = exchange(sent_ref, gotx_ref, x_send, x_recv)
    more_cot()
    gotx_ref[me] = sent_ref[me]
    for load in loads:
        load.wait()

    o1 = (o1_ref[0], o1_ref[1])
    o1b = (o1b_ref[0], o1b_ref[1])
    i2 = (i2_ref[0], i2_ref[1])
    i2b = (i2b_ref[0], i2b_ref[1])
    tcos = tc_ref[...]
    tsin = ts_ref[...]

    def gathered(ref):
        cols = []
        whole = [ref[d].astype(f32) for d in range(count)]
        for c in range(chans):
            tiles = []
            for d in range(count):
                at = c * th
                for h in range(per):
                    tiles.append(whole[d][at : at + th, h * lanes : (h + 1) * lanes])
            cols.append(jnp.concatenate(tiles, axis=0))
        return jnp.concatenate(cols, axis=1)

    def forward(first):
        wide = []
        for c in range(chans):
            fr = first[:rows, c * lanes : (c + 1) * lanes]
            fi = first[rows:, c * lanes : (c + 1) * lanes]
            wide.append(jnp.concatenate([fr * tcos + fi * tsin, fi * tcos - fr * tsin], axis=1))
        spec = dot_split(split(jnp.concatenate(wide, axis=0)), i2)
        return spec[:, :lanes], spec[:, lanes:]

    def backward(sr, si):
        back = dot_split(split(jnp.concatenate([sr, si], axis=1)), i2b)
        cols = []
        for c in range(chans):
            br = back[c * rows : (c + 1) * rows, :lanes]
            bi = back[c * rows : (c + 1) * rows, lanes:]
            cols.append(jnp.concatenate([br * tcos - bi * tsin, bi * tcos + br * tsin], axis=0))
        return dot_split(o1b, split(jnp.concatenate(cols, axis=1))) * (1.0 / waves)

    def spread(at):
        flat = jnp.concatenate([resp_ref[at, c].T for c in range(chans)], axis=0)
        return jnp.broadcast_to(flat[:, None, :], (flat.shape[0], th, lanes)).reshape(
            flat.shape[0] * th, lanes
        )

    resp_r = spread(0)
    resp_i = spread(1)
    end_conv()
    x = gathered(gotx_ref).astype(bf16)
    sr, si = forward(dot(o1[0], x) + dot(o1[1], x))
    v = backward(resp_r * sr - resp_i * si, resp_r * si + resp_i * sr)
    slope = 0.5 * (1.0 + lax.erf(v * inv_root_two)) + v * jnp.exp(-0.5 * v * v) * inv_root_tau
    end_cot()
    g = gathered(gotc_ref) * slope
    gr, gi = forward(dot_split(o1, split(g)))
    scale = 1.0 / waves
    y = backward(resp_r * gr + resp_i * gi, resp_r * gi - resp_i * gr)
    for d in range(count):
        blocks = []
        for c in range(chans):
            col = y[:, c * lanes : (c + 1) * lanes]
            tiles = [col[(d * per + h) * th : (d * per + h + 1) * th] for h in range(per)]
            blocks.append(jnp.concatenate(tiles, axis=1))
        back_ref[d] = jnp.concatenate(blocks, axis=0).astype(bf16)
    end_grad = exchange(back_ref, grad_ref, g_send, g_recv)
    grad_ref[me] = back_ref[me]
    scale = 1.0 / waves
    crosses = (sr * gr + si * gi, sr * gi - si * gr)
    for at, cross in enumerate(crosses):
        summed = jnp.sum(cross.reshape(chans * outer, th, lanes), axis=1) * scale
        for c in range(chans):
            fg_ref[at, c] = summed[c * outer : (c + 1) * outer].T
    v_ref[...] = jnp.zeros(v_ref.shape, f32)
    for ps in range(2):
        for pm in range(2):
            for ti in range(3):
                i = (None, 3, 1)[ti] if ps else 4 - 2 * ti
                for sh in range(3):
                    j = 2 * sh + pm
                    if i is not None and j < ks:
                        row = (ps * 2 + pm) * cin
                        col = (ti * 3 + sh) * cout
                        at = (i * ks + j) * cin
                        v_ref[row : row + cin, col : col + cout] = w_ref[at : at + cin, :].astype(f32)
    end_grad()

    g_all = grad_ref[...].reshape(cout * th, half)
    gt_ref[...] = dot(swap_rows(th, cout), g_all).astype(bf16)
    g_right = remote(
        gt_ref.at[:, half - lanes : half], glo_ref, halo_send.at[2], halo_recv.at[2], peer_of(1)
    )
    g_left = remote(
        gt_ref.at[:, 0:lanes], ghi_ref, halo_send.at[3], halo_recv.at[3], peer_of(count - 1)
    )
    g_right.start()
    g_left.start()
    total = None
    for t in range(th):
        term = lax.dot_general(
            gt_ref[t * cout : (t + 1) * cout, :],
            pp_ref[t * step : t * step + taps_rows, :],
            (((1,), (1,)), ((), ())),
            preferred_element_type=f32,
        )
        total = term if total is None else total + term
    part_width = part_ref.shape[2]
    total = jnp.concatenate(
        [total, jnp.zeros((cout, cuts * part_width - taps_rows), f32)], axis=1
    )
    for r in range(cout // 16):
        for p in range(cuts):
            part_ref[r * cuts + p] = total[
                r * 16 : (r + 1) * 16, p * part_width : (p + 1) * part_width
            ].astype(bf16)
    end_terms = exchange(part_ref, term_ref, t_send, t_recv)
    term_ref[me] = part_ref[me]

    blank = jnp.zeros((3 * cout, half), bf16)
    gg_ref[0 : 3 * cout, :] = blank
    gg_ref[(th + 1) * 3 * cout : (th + 2) * 3 * cout, :] = blank
    p = lax.broadcasted_iota(jnp.int32, (1, half), 1)
    g2 = gt_ref[...]
    g_right.wait()
    g_left.wait()
    for sh in range(3):
        if sh == 0:
            rim = jnp.where((p == half - 1) & (me < count - 1), 0, -1)
            moved = dot(g2, one_hot(half, half, p + 1))
            moved = (moved + dot(ghi_ref[...], one_hot(lanes, half, rim))).astype(bf16)
        elif sh == 1:
            moved = g2
        else:
            rim = jnp.where((p == 0) & (me > 0), lanes - 1, -1)
            moved = dot(g2, one_hot(half, half, p - 1))
            moved = (moved + dot(glo_ref[...], one_hot(lanes, half, rim))).astype(bf16)
        for t in range(th):
            at = ((t + 1) * 3 + sh) * cout
            gg_ref[at : at + cout, :] = moved[t * cout : (t + 1) * cout, :]

    end_terms()
    whole_ref[me] = (
        jnp.sum(term_ref[...].astype(f32), axis=0) * (1.0 / math.sqrt(th * waves))
    ).astype(bf16)

    def share(k):
        return remote(whole_ref.at[me], whole_ref.at[me], w_send.at[k], w_recv.at[k], peer_of(k))

    def share_start(k, carry):
        share(k).start()
        return carry

    def share_end(k, carry):
        share(k).wait()
        return carry

    lax.fori_loop(1, count, share_start, 0)

    weights = v_ref[...].astype(bf16)
    for q in range(th):
        dx = dot(weights, gg_ref[q * 3 * cout : (q + 3) * 3 * cout, :]).astype(bf16)
        for ps in range(2):
            for pm in range(2):
                at = (ps * 2 + pm) * cin
                row = (2 * q + ps) * cin
                xo_ref[row : row + cin, pm * half : (pm + 1) * half] = dx[at : at + cin, :]
    m = lax.broadcasted_iota(jnp.int32, (1, width), 1)
    weave = one_hot(width, width, (m & 1) * half + (m >> 1))
    woven = dot(xo_ref[...], weave).astype(bf16)
    dx_ref[...] = dot(swap_rows(cin, tw), woven).astype(bf16)
    lax.fori_loop(1, count, share_end, 0)
    tap_ref[...] = whole_ref[...].astype(f32)


def per_device(signal, conv_taps, response, cotangent):
    ks, _, cout, cin = conv_taps.shape
    tw, width = signal.shape[1:]
    th, half = cotangent.shape[1:]
    count = lax.axis_size("fibre")
    chans = response.shape[1]
    waves = response.shape[2]
    outer = waves // lanes
    group = chans * th
    taps_rows = ks * ks * cin
    parts = count * 16 // cout
    assert parts * cout == count * 16
    part_width = -(-taps_rows // (parts * lanes)) * lanes
    shape = jax.ShapeDtypeStruct
    taps_flat = conv_taps.transpose(0, 1, 3, 2).reshape(taps_rows, cout)
    tables = dft_tables(outer, th)
    dims = (cin, tw, ks, cout, th, chans, count, parts)

    def body(*refs):
        section_kernel(dims, *refs)

    vmem = pl.BlockSpec(memory_space=pltpu.VMEM)
    every = pltpu.SemaphoreType.DMA((count,))
    dx, fgrad, taps = pl.pallas_call(
        body,
        out_shape=[
            shape((cin * tw, width), bf16),
            shape((2, chans, lanes, outer), f32),
            shape((count, 16, part_width), f32),
        ],
        in_specs=[vmem] * 4 + [pl.BlockSpec(memory_space=pl.ANY)] * 6,
        out_specs=[vmem] * 3,
        scratch_shapes=[pltpu.VMEM(table.shape, table.dtype) for table in tables]
        + [
            pltpu.VMEM((cin * tw, lanes), bf16),
            pltpu.VMEM((cin * tw, lanes), bf16),
            pltpu.VMEM(((tw + 4) * ks * cin, half), bf16),
            pltpu.VMEM((cout * th, half), bf16),
            pltpu.VMEM((count, group, half), bf16),
            pltpu.VMEM((count, group, half), bf16),
            pltpu.VMEM((count, group, half), bf16),
            pltpu.VMEM((count, group, half), bf16),
            pltpu.VMEM((count, group, half), bf16),
            pltpu.VMEM((cout * th, half), bf16),
            pltpu.VMEM(((th + 2) * 3 * cout, half), bf16),
            pltpu.VMEM((cin * tw, width), bf16),
            pltpu.VMEM((count, 16, part_width), bf16),
            pltpu.VMEM((count, 16, part_width), bf16),
            pltpu.VMEM((count, 16, part_width), bf16),
            pltpu.VMEM((cout * th, lanes), bf16),
            pltpu.VMEM((cout * th, lanes), bf16),
            pltpu.VMEM((4 * cin, 9 * cout), f32),
            pltpu.SemaphoreType.DMA((6,)),
            pltpu.SemaphoreType.DMA((4,)),
            pltpu.SemaphoreType.DMA((4,)),
        ]
        + [every] * 10,
        compiler_params=pltpu.CompilerParams(
            vmem_limit_bytes=vmem_bytes, collective_id=0, has_side_effects=True
        ),
        cost_estimate=pl.CostEstimate(
            flops=6000000000, bytes_accessed=8000000, transcendentals=0
        ),
    )(
        signal.reshape(cin * tw, width),
        cotangent.reshape(count, group, half),
        taps_flat,
        response.reshape(2, chans, lanes, outer),
        *tables,
    )
    filter_grad = fgrad.reshape(2, chans, waves)
    tap_grad = (
        taps.reshape(cout // 16, parts, 16, part_width)
        .transpose(0, 2, 1, 3)
        .reshape(cout, parts * part_width)[:, :taps_rows]
        .reshape(cout, ks, ks, cin)
        .transpose(1, 2, 0, 3)
    )
    return (dx.reshape(signal.shape), tap_grad, filter_grad)


def solution(mesh):
    in_specs = (P("parts", None, "fibre"), P(), P(None, "fibre", None), P("parts", None, "fibre"))
    out_specs = (P("parts", None, "fibre"), P("parts", None, None, None), P("parts", "fibre", None))
    return jax.shard_map(
        per_device, mesh=mesh, in_specs=in_specs, out_specs=out_specs, check_vma=False
    )
```

```python
import math

import jax
import jax.numpy as jnp
import numpy as np
from jax import lax
from jax.experimental import pallas as pl
from jax.experimental.pallas import tpu as pltpu
from jax.sharding import PartitionSpec as P

inv_root_two = 1.0 / math.sqrt(2.0)
inv_root_tau = 1.0 / math.sqrt(2.0 * math.pi)
lanes = 128
f32 = jnp.float32
bf16 = jnp.bfloat16
vmem_bytes = 50 * 1024 * 1024


def log2(size):
    bits = size.bit_length() - 1
    assert 1 << bits == size
    return bits


def dot(left, right):
    return jnp.dot(left, right, preferred_element_type=f32)


def one_hot(rows, cols, wanted):
    axis = 0 if wanted.shape[0] == 1 else 1
    index = lax.broadcasted_iota(jnp.int32, (rows, cols), axis)
    return jnp.where(index == wanted, 1.0, 0.0).astype(bf16)


def swap_rows(outer, inner):
    count = outer * inner
    row = lax.broadcasted_iota(jnp.int32, (count, 1), 0)
    source = (row & (inner - 1)) * outer + (row >> log2(inner))
    return one_hot(count, count, source)


def split(values):
    high = values.astype(bf16)
    return high, (values - high.astype(f32)).astype(bf16)


def dot_split(left, right):
    return dot(left[0], right[0]) + (dot(left[0], right[1]) + dot(left[1], right[0]))


def dft_tables(outer, th):
    waves = outer * lanes
    turn = 2.0 * math.pi
    a = np.arange(outer)
    b = np.arange(lanes)
    ang = turn * ((a[:, None] * a[None, :]) % outer) / outer
    eye = np.eye(th)
    o1 = np.concatenate([np.kron(np.cos(ang), eye), -np.kron(np.sin(ang), eye)], axis=0)
    ang = turn * ((b[:, None] * b[None, :]) % lanes) / lanes
    i2 = np.block([[np.cos(ang), -np.sin(ang)], [np.sin(ang), np.cos(ang)]])
    ang = np.repeat(turn * (a[:, None] * b[None, :]) / waves, th, axis=0)

    def halves(table):
        table = table.astype(np.float32)
        high = table.astype(bf16)
        return np.stack([high, (table - high.astype(np.float32)).astype(bf16)])

    return (
        halves(o1),
        halves(o1.T),
        halves(i2),
        halves(i2.T),
        np.cos(ang).astype(np.float32),
        np.sin(ang).astype(np.float32),
    )


MESH = pl.DeviceIdType.MESH


def section_kernel(dims, *refs):
    (cin, tw, ks, cout, th, chans, count, cuts) = dims
    (x_ref, cot_ref, w_ref, resp_ref) = refs[:4]
    table_refs = refs[4:10]
    (dx_ref, fg_ref, tap_ref) = refs[10:13]
    (o1_ref, o1b_ref, i2_ref, i2b_ref, tc_ref, ts_ref) = held = refs[13:19]
    (lo_ref, hi_ref, pp_ref, ct_ref, sent_ref, gotx_ref, gotc_ref) = refs[19:26]
    (back_ref, grad_ref, gt_ref, gg_ref, xo_ref, part_ref, term_ref, whole_ref) = refs[26:34]
    (glo_ref, ghi_ref, v_ref) = refs[34:37]
    (table_sem, halo_send, halo_recv, c_send, c_recv, x_send, x_recv) = refs[37:44]
    (g_send, g_recv, t_send, t_recv, w_send, w_recv) = refs[44:50]
    me = lax.axis_index("fibre")
    width = x_ref.shape[1]
    half = width // 2
    per = half // lanes
    outer = count * per
    rows = outer * th
    waves = outer * lanes
    group = chans * th

    def peer_of(k):
        return lax.rem(me + k, count)

    barrier = pltpu.get_barrier_semaphore()

    def greet(k, carry):
        pl.semaphore_signal(
            barrier, inc=1, device_id={"fibre": peer_of(k)}, device_id_type=MESH
        )
        return carry

    lax.fori_loop(1, count, greet, 0)
    loads = [
        pltpu.make_async_copy(src, dst, table_sem.at[i])
        for i, (src, dst) in enumerate(zip(table_refs, held))
    ]
    for load in loads:
        load.start()
    pl.semaphore_wait(barrier, count - 1)

    def remote(src, dst, ssem, rsem, peer):
        return pltpu.make_async_remote_copy(
            src_ref=src,
            dst_ref=dst,
            send_sem=ssem,
            recv_sem=rsem,
            device_id={"fibre": peer},
            device_id_type=MESH,
        )

    def exchange(src, dst, ssem, rsem, last=count):
        def copy(k):
            peer = peer_of(k)
            return remote(src.at[peer], dst.at[me], ssem.at[k], rsem.at[k], peer)

        def go(k, carry):
            copy(k).start()
            return carry

        def end(k, carry):
            copy(k).wait()
            return carry

        lax.fori_loop(1, last, go, 0)
        rest = lambda: lax.fori_loop(last, count, go, 0)
        finish = lambda: lax.fori_loop(1, count, end, 0)
        return (rest, finish) if last < count else finish

    to_right = remote(
        x_ref.at[:, width - lanes : width], lo_ref, halo_send.at[0], halo_recv.at[0], peer_of(1)
    )
    to_left = remote(
        x_ref.at[:, 0:lanes], hi_ref, halo_send.at[1], halo_recv.at[1], peer_of(count - 1)
    )
    to_right.start()
    to_left.start()
    more_cot, end_cot = exchange(cot_ref, gotc_ref, c_send, c_recv, count // 2)
    gotc_ref[me] = cot_ref[me]

    order = swap_rows(tw, cin)
    x2 = dot(order, x_ref[...]).astype(bf16)
    blank = jnp.zeros((2 * ks * cin, half), bf16)
    pp_ref[0 : 2 * ks * cin, :] = blank
    pp_ref[(tw + 2) * ks * cin : (tw + 4) * ks * cin, :] = blank
    to_right.wait()
    to_left.wait()
    lo2 = dot(order, lo_ref[...]).astype(bf16)
    hi2 = dot(order, hi_ref[...]).astype(bf16)
    for j in range(ks):
        m = 2 * lax.broadcasted_iota(jnp.int32, (1, half), 1) + (j - 2)
        pj = dot(x2, one_hot(width, half, m))
        if j < 2:
            pj += dot(lo2, one_hot(lanes, half, jnp.where((m < 0) & (me > 0), lanes + m, -1)))
        if j > 3:
            inside = (m >= width) & (me < count - 1)
            pj += dot(hi2, one_hot(lanes, half, jnp.where(inside, m - width, -1)))
        pj = pj.astype(bf16)
        for s in range(tw):
            at = ((s + 2) * ks + j) * cin
            pp_ref[at : at + cin, :] = pj[s * cin : (s + 1) * cin, :]
    step = 2 * ks * cin
    taps_rows = ks * ks * cin
    for t in range(th):
        patches = pp_ref[t * step : t * step + taps_rows, :]
        ct_ref[t * cout : (t + 1) * cout, :] = lax.dot_general(
            w_ref[...], patches, (((0,), (0,)), ((), ())), preferred_element_type=f32
        ).astype(bf16)
    conv_out = dot(swap_rows(cout, th), ct_ref[...]).astype(bf16)
    sent_ref[...] = conv_out.reshape(count, group, half)
    end_conv = exchange(sent_ref, gotx_ref, x_send, x_recv)
    more_cot()
    gotx_ref[me] = sent_ref[me]
    for load in loads:
        load.wait()

    o1 = (o1_ref[0], o1_ref[1])
    o1b = (o1b_ref[0], o1b_ref[1])
    i2 = (i2_ref[0], i2_ref[1])
    i2b = (i2b_ref[0], i2b_ref[1])
    tcos = tc_ref[...]
    tsin = ts_ref[...]

    def gathered(ref):
        cols = []
        whole = [ref[d].astype(f32) for d in range(count)]
        for c in range(chans):
            tiles = []
            for d in range(count):
                at = c * th
                for h in range(per):
                    tiles.append(whole[d][at : at + th, h * lanes : (h + 1) * lanes])
            cols.append(jnp.concatenate(tiles, axis=0))
        return jnp.concatenate(cols, axis=1)

    def forward(first):
        wide = []
        for c in range(chans):
            fr = first[:rows, c * lanes : (c + 1) * lanes]
            fi = first[rows:, c * lanes : (c + 1) * lanes]
            wide.append(jnp.concatenate([fr * tcos + fi * tsin, fi * tcos - fr * tsin], axis=1))
        spec = dot_split(split(jnp.concatenate(wide, axis=0)), i2)
        return spec[:, :lanes], spec[:, lanes:]

    def backward(sr, si):
        back = dot_split(split(jnp.concatenate([sr, si], axis=1)), i2b)
        cols = []
        for c in range(chans):
            br = back[c * rows : (c + 1) * rows, :lanes]
            bi = back[c * rows : (c + 1) * rows, lanes:]
            cols.append(jnp.concatenate([br * tcos - bi * tsin, bi * tcos + br * tsin], axis=0))
        return dot_split(o1b, split(jnp.concatenate(cols, axis=1))) * (1.0 / waves)

    def spread(at):
        flat = jnp.concatenate([resp_ref[at, c].T for c in range(chans)], axis=0)
        return jnp.broadcast_to(flat[:, None, :], (flat.shape[0], th, lanes)).reshape(
            flat.shape[0] * th, lanes
        )

    resp_r = spread(0)
    resp_i = spread(1)
    end_conv()
    x = gathered(gotx_ref).astype(bf16)
    sr, si = forward(dot(o1[0], x) + dot(o1[1], x))
    v = backward(resp_r * sr - resp_i * si, resp_r * si + resp_i * sr)
    slope = 0.5 * (1.0 + lax.erf(v * inv_root_two)) + v * jnp.exp(-0.5 * v * v) * inv_root_tau
    end_cot()
    g = gathered(gotc_ref) * slope
    gr, gi = forward(dot_split(o1, split(g)))
    scale = 1.0 / waves
    y = backward(resp_r * gr + resp_i * gi, resp_r * gi - resp_i * gr)
    for d in range(count):
        blocks = []
        for c in range(chans):
            col = y[:, c * lanes : (c + 1) * lanes]
            tiles = [col[(d * per + h) * th : (d * per + h + 1) * th] for h in range(per)]
            blocks.append(jnp.concatenate(tiles, axis=1))
        back_ref[d] = jnp.concatenate(blocks, axis=0).astype(bf16)
    end_grad = exchange(back_ref, grad_ref, g_send, g_recv)
    grad_ref[me] = back_ref[me]
    scale = 1.0 / waves
    crosses = (sr * gr + si * gi, sr * gi - si * gr)
    for at, cross in enumerate(crosses):
        summed = jnp.sum(cross.reshape(chans * outer, th, lanes), axis=1) * scale
        for c in range(chans):
            fg_ref[at, c] = summed[c * outer : (c + 1) * outer].T
    v_ref[...] = jnp.zeros(v_ref.shape, f32)
    for ps in range(2):
        for pm in range(2):
            for ti in range(3):
                i = (None, 3, 1)[ti] if ps else 4 - 2 * ti
                for sh in range(3):
                    j = 2 * sh + pm
                    if i is not None and j < ks:
                        row = (ps * 2 + pm) * cin
                        col = (ti * 3 + sh) * cout
                        at = (i * ks + j) * cin
                        v_ref[row : row + cin, col : col + cout] = w_ref[at : at + cin, :].astype(f32)
    end_grad()

    g_all = grad_ref[...].reshape(cout * th, half)
    gt_ref[...] = dot(swap_rows(th, cout), g_all).astype(bf16)
    g_right = remote(
        gt_ref.at[:, half - lanes : half], glo_ref, halo_send.at[2], halo_recv.at[2], peer_of(1)
    )
    g_left = remote(
        gt_ref.at[:, 0:lanes], ghi_ref, halo_send.at[3], halo_recv.at[3], peer_of(count - 1)
    )
    g_right.start()
    g_left.start()
    total = None
    for t in range(th):
        term = lax.dot_general(
            gt_ref[t * cout : (t + 1) * cout, :],
            pp_ref[t * step : t * step + taps_rows, :],
            (((1,), (1,)), ((), ())),
            preferred_element_type=f32,
        )
        total = term if total is None else total + term
    part_width = part_ref.shape[2]
    total = jnp.concatenate(
        [total, jnp.zeros((cout, cuts * part_width - taps_rows), f32)], axis=1
    )
    for r in range(cout // 16):
        for p in range(cuts):
            part_ref[r * cuts + p] = total[
                r * 16 : (r + 1) * 16, p * part_width : (p + 1) * part_width
            ].astype(bf16)
    end_terms = exchange(part_ref, term_ref, t_send, t_recv)
    term_ref[me] = part_ref[me]

    blank = jnp.zeros((3 * cout, half), bf16)
    gg_ref[0 : 3 * cout, :] = blank
    gg_ref[(th + 1) * 3 * cout : (th + 2) * 3 * cout, :] = blank
    p = lax.broadcasted_iota(jnp.int32, (1, half), 1)
    g2 = gt_ref[...]
    g_right.wait()
    g_left.wait()
    for sh in range(3):
        if sh == 0:
            rim = jnp.where((p == half - 1) & (me < count - 1), 0, -1)
            moved = dot(g2, one_hot(half, half, p + 1))
            moved = (moved + dot(ghi_ref[...], one_hot(lanes, half, rim))).astype(bf16)
        elif sh == 1:
            moved = g2
        else:
            rim = jnp.where((p == 0) & (me > 0), lanes - 1, -1)
            moved = dot(g2, one_hot(half, half, p - 1))
            moved = (moved + dot(glo_ref[...], one_hot(lanes, half, rim))).astype(bf16)
        for t in range(th):
            at = ((t + 1) * 3 + sh) * cout
            gg_ref[at : at + cout, :] = moved[t * cout : (t + 1) * cout, :]

    end_terms()
    whole_ref[me] = (
        jnp.sum(term_ref[...].astype(f32), axis=0) * (1.0 / math.sqrt(th * waves))
    ).astype(bf16)

    def share(k):
        return remote(whole_ref.at[me], whole_ref.at[me], w_send.at[k], w_recv.at[k], peer_of(k))

    def share_start(k, carry):
        share(k).start()
        return carry

    def share_end(k, carry):
        share(k).wait()
        return carry

    lax.fori_loop(1, count, share_start, 0)

    weights = v_ref[...].astype(bf16)
    for q in range(th):
        dx = dot(weights, gg_ref[q * 3 * cout : (q + 3) * 3 * cout, :]).astype(bf16)
        for ps in range(2):
            for pm in range(2):
                at = (ps * 2 + pm) * cin
                row = (2 * q + ps) * cin
                xo_ref[row : row + cin, pm * half : (pm + 1) * half] = dx[at : at + cin, :]
    m = lax.broadcasted_iota(jnp.int32, (1, width), 1)
    weave = one_hot(width, width, (m & 1) * half + (m >> 1))
    woven = dot(xo_ref[...], weave).astype(bf16)
    dx_ref[...] = dot(swap_rows(cin, tw), woven).astype(bf16)
    lax.fori_loop(1, count, share_end, 0)
    tap_ref[...] = whole_ref[...].astype(f32)


def per_device(signal, conv_taps, response, cotangent):
    ks, _, cout, cin = conv_taps.shape
    tw, width = signal.shape[1:]
    th, half = cotangent.shape[1:]
    count = lax.axis_size("fibre")
    chans = response.shape[1]
    waves = response.shape[2]
    outer = waves // lanes
    group = chans * th
    taps_rows = ks * ks * cin
    parts = count * 16 // cout
    assert parts * cout == count * 16
    part_width = -(-taps_rows // (parts * lanes)) * lanes
    shape = jax.ShapeDtypeStruct
    taps_flat = conv_taps.transpose(0, 1, 3, 2).reshape(taps_rows, cout)
    tables = dft_tables(outer, th)
    dims = (cin, tw, ks, cout, th, chans, count, parts)

    def body(*refs):
        section_kernel(dims, *refs)

    vmem = pl.BlockSpec(memory_space=pltpu.VMEM)
    every = pltpu.SemaphoreType.DMA((count,))
    dx, fgrad, taps = pl.pallas_call(
        body,
        out_shape=[
            shape((cin * tw, width), bf16),
            shape((2, chans, lanes, outer), f32),
            shape((count, 16, part_width), f32),
        ],
        in_specs=[vmem] * 4 + [pl.BlockSpec(memory_space=pltpu.HBM)] * 6,
        out_specs=[vmem] * 3,
        scratch_shapes=[pltpu.VMEM(table.shape, table.dtype) for table in tables]
        + [
            pltpu.VMEM((cin * tw, lanes), bf16),
            pltpu.VMEM((cin * tw, lanes), bf16),
            pltpu.VMEM(((tw + 4) * ks * cin, half), bf16),
            pltpu.VMEM((cout * th, half), bf16),
            pltpu.VMEM((count, group, half), bf16),
            pltpu.VMEM((count, group, half), bf16),
            pltpu.VMEM((count, group, half), bf16),
            pltpu.VMEM((count, group, half), bf16),
            pltpu.VMEM((count, group, half), bf16),
            pltpu.VMEM((cout * th, half), bf16),
            pltpu.VMEM(((th + 2) * 3 * cout, half), bf16),
            pltpu.VMEM((cin * tw, width), bf16),
            pltpu.VMEM((count, 16, part_width), bf16),
            pltpu.VMEM((count, 16, part_width), bf16),
            pltpu.VMEM((count, 16, part_width), bf16),
            pltpu.VMEM((cout * th, lanes), bf16),
            pltpu.VMEM((cout * th, lanes), bf16),
            pltpu.VMEM((4 * cin, 9 * cout), f32),
            pltpu.SemaphoreType.DMA((6,)),
            pltpu.SemaphoreType.DMA((4,)),
            pltpu.SemaphoreType.DMA((4,)),
        ]
        + [every] * 10,
        compiler_params=pltpu.CompilerParams(
            vmem_limit_bytes=vmem_bytes, collective_id=0, has_side_effects=True
        ),
        cost_estimate=pl.CostEstimate(
            flops=6000000000, bytes_accessed=8000000, transcendentals=0
        ),
    )(
        signal.reshape(cin * tw, width),
        cotangent.reshape(count, group, half),
        taps_flat,
        response.reshape(2, chans, lanes, outer),
        *tables,
    )
    filter_grad = fgrad.reshape(2, chans, waves)
    tap_grad = (
        taps.reshape(cout // 16, parts, 16, part_width)
        .transpose(0, 2, 1, 3)
        .reshape(cout, parts * part_width)[:, :taps_rows]
        .reshape(cout, ks, ks, cin)
        .transpose(1, 2, 0, 3)
    )
    return (dx.reshape(signal.shape), tap_grad, filter_grad)


def solution(mesh):
    in_specs = (P("parts", None, "fibre"), P(), P(None, "fibre", None), P("parts", None, "fibre"))
    out_specs = (P("parts", None, "fibre"), P("parts", None, None, None), P("parts", "fibre", None))
    return jax.shard_map(
        per_device, mesh=mesh, in_specs=in_specs, out_specs=out_specs, check_vma=False
    )
```
